512 devices in a mesh: date: 8 (over z_lo), tile: 64 (over z_hi, y, x, core).
Axes of the slice: x: 4, y: 4, z: 16 (z_hi: 2, z_lo: 8; z = z_hi * 8 + z_lo), core: 2. Of those that a mesh axis runs over, the one named last changes fastest.
Arguments:
- reflectance: bfloat16 [72, 10, 512, 1024], P('date', None, 'tile'), may hold values from 0 to 0.59765625
- clear_mask: int32 [72, 512, 1024], P('date', 'tile'), may hold values from 0 to 1, as said below
- time_kernel: float32 [5], replicated, may hold values from 0.25 to 1
- space_kernel: float32 [5], replicated, may hold values from 0.25 to 1
Outputs:
- filled_bands: bfloat16 [72, 10, 512, 1024], P('date', None, 'tile')
- coefficients: float32 [12, 24, 512, 1024], P(None, None, 'tile', 'date')
The draws below stay inside these ranges and needn't reach their ends.
Inputs may be any that keep to these rules, and one draw needn't show every extreme that they name: `clear_mask`: cloud cover differs strongly between strips of 8 rows and between dates.
All inputs are finite; a program needn't handle non-finite values.
Results may differ from the reference program's by a relative error of at most 0.0065.
Values may be sent and summed in bfloat16 or wider, within the bound.
A program may use at most 128 MiB of HBM per device.

```python
import math
import jax
import jax.numpy as jnp
from jax import lax

DATES = 72
BANDS = 10
TERMS = 24
ROWS_DEV = 8
COLS = 1024
H = 512


def draw_clear_mask(key, part):
    key = jax.random.fold_in(key, 11)
    first, second = jax.random.split(key)
    strips = H // ROWS_DEV
    level = jax.random.randint(first, (DATES, strips, 1, 1), 0, 100)
    percent = level * level // 100
    rolled = jax.random.randint(second, (DATES, strips, ROWS_DEV, COLS), 0, 100)
    clear = (rolled >= percent).astype(jnp.int32)
    return clear.reshape(DATES, H, COLS)


def level_of(rng, shape, cuts, least, high):
    level, own = 1.0, jax.random.fold_in(rng, 6)
    for position, parts in cuts:
        draws = jnp.exp(jax.random.uniform(jax.random.fold_in(own, position), (parts,), jnp.float32, least / len(cuts), high / len(cuts)))
        level = level * jnp.repeat(draws, shape[position] // parts).reshape([-1 if axis == position else 1 for axis in range(len(shape))])
    return level


def setup_inputs(seed: int = 0) -> dict:
    streams_of = jax.random.split(jax.random.key(seed), 5)
    return {
        "reflectance": jnp.clip(0.59765625 * jax.random.uniform(streams_of[0], (DATES, BANDS, H, COLS), jnp.float32) ** level_of(streams_of[0], (DATES, BANDS, H, COLS), ((0, 8), (2, 64)), -0.2, 0.2), 0.0, 0.59765625).astype(jnp.bfloat16),
        "clear_mask": draw_clear_mask(jax.random.fold_in(streams_of[4], 71), 0),
        "time_kernel": jnp.clip(jnp.exp(jax.random.uniform(streams_of[2], (5,), jnp.float32, math.log(0.25), math.log(1.0))), 0.25, 1.0),
        "space_kernel": jnp.clip(jnp.exp(jax.random.uniform(streams_of[3], (5,), jnp.float32, math.log(0.25), math.log(1.0))), 0.25, 1.0),
    }


def fit_matrix(dates, terms):
    steps = jnp.arange(dates, dtype=jnp.float32)
    columns = [jnp.ones((dates,), jnp.float32), steps / dates - 0.5]
    for order in range(1, (terms - 2) // 2 + 1):
        angle = 2.0 * math.pi * order * steps / dates
        columns.append(jnp.cos(angle))
        columns.append(jnp.sin(angle))
    basis = jnp.stack(columns, axis=1)
    gram = jnp.dot(basis.T, basis, precision=lax.Precision.HIGHEST)
    factor = jnp.linalg.cholesky(gram)
    return jax.scipy.linalg.cho_solve((factor, True), basis.T)

def smooth(field, time_kernel, space_kernel):
    dates, rows, cols = field.shape
    padded = jnp.pad(field, 2)
    timed = sum((time_kernel[i] * padded[i:i + dates] for i in range(5)))
    rowed = sum((space_kernel[j] * timed[:, j:j + rows] for j in range(5)))
    return sum((space_kernel[k] * rowed[:, :, k:k + cols] for k in range(5)))

def reference(reflectance, clear_mask, time_kernel, space_kernel):
    clear = clear_mask.astype(jnp.float32)
    weight_total = smooth(clear, time_kernel, space_kernel)

    def one_band(band):
        values = band.astype(jnp.float32)
        weighted_sum = smooth(clear * values, time_kernel, space_kernel)
        return (clear * values + (1.0 - clear) * weighted_sum / (weight_total + 1.0)).astype(jnp.bfloat16)
    filled = lax.map(one_band, jnp.moveaxis(reflectance, 1, 0))
    red = filled[2].astype(jnp.float32)
    near = filled[6].astype(jnp.float32)
    swir = filled[8].astype(jnp.float32)
    savi = (1.5 * (near - red) / (near + red + 0.5)).astype(jnp.bfloat16)
    moisture = ((near - swir) / (near + swir + 0.5)).astype(jnp.bfloat16)
    series = jnp.concatenate([filled, savi[None], moisture[None]], axis=0)
    fitting = fit_matrix(series.shape[1], TERMS)

    def one_channel(channel):
        return jnp.einsum('kt,thw->khw', fitting, channel.astype(jnp.float32), precision=lax.Precision.HIGHEST)
    coefficients = lax.map(one_channel, series)
    return (jnp.moveaxis(filled, 0, 1), coefficients)
```

```python
import functools
import math

import jax
import jax.numpy as jnp
import numpy as np
from jax import lax
from jax.experimental import pallas as pl
from jax.experimental.pallas import tpu as pltpu
from jax.sharding import PartitionSpec as P

TERMS = 24
PACK = 32
AHEAD = 4
MESH = pl.DeviceIdType.MESH
F32 = jnp.float32
BF16 = jnp.bfloat16


def fit_matrix(dates, terms):
    steps = np.arange(dates, dtype=np.float64)
    columns = [np.ones((dates,)), steps / dates - 0.5]
    for order in range(1, (terms - 2) // 2 + 1):
        angle = 2.0 * math.pi * order * steps / dates
        columns.append(np.cos(angle))
        columns.append(np.sin(angle))
    basis = np.stack(columns, axis=1)
    factor = np.linalg.cholesky(basis.T @ basis)
    return np.linalg.solve(factor.T, np.linalg.solve(factor, basis.T))


def fit_operand(dates, rows):
    wide = np.kron(fit_matrix(dates, TERMS), np.eye(rows)).astype(np.float32)
    high = wide.astype(BF16)
    rest = (wide - high.astype(np.float32)).astype(BF16)
    return np.concatenate([high, rest], axis=0)


def own_order(dates):
    return [0, 1, dates - 2, dates - 1] + list(range(2, dates - 2))


def strip_rows(n, dates):
    q = n >> 3
    date = jnp.where(q < 4 + dates, q - 6, -100)
    date = jnp.where(q < 8, q - 8 + dates, date)
    date = jnp.where(q < 6, q - 4, date)
    date = jnp.where(q < 4, q - 2 + dates, date)
    date = jnp.where(q < 2, q - 2, date)
    return date, n & 7


def halo_rows(m, dates, low, high):
    at = m & (PACK - 1)
    date = jnp.where(at < 2 * (dates + 4), (at >> 1) - 2, -200)
    return date, (at & 1) + jnp.where(m < PACK, low, high)


def kernel(
    sizes,
    refl, mask, time_k, space_k, fit_in,
    filled, coef,
    raw, cloud, fit, chan, packed, gain, out, got, result, smooth_m, select_m,
    in_sem, date_send, date_recv, row_send, row_recv, all_send, all_recv, fill_sem, coef_sem,
):
    nd, nt, dates, bands, rows, cols = sizes
    width = cols // nd
    own = dates * rows
    strip = 4 * rows + own + rows
    total = strip + 2 * PACK
    day = lax.axis_index("date")
    tile = lax.axis_index("tile")
    has_low, has_high = day > 0, day < nd - 1
    has_up, has_down = tile > 0, tile < nt - 1

    def band_in(b):
        return pltpu.make_async_copy(refl.at[:, b], raw.at[b], in_sem.at[b])

    mask_in = pltpu.make_async_copy(mask, cloud, in_sem.at[bands])
    fit_copy = pltpu.make_async_copy(fit_in, fit, in_sem.at[bands + 1])
    mask_in.start()

    @pl.loop(0, bands)
    def _(b):
        band_in(b).start()

    fit_copy.start()

    barrier = pltpu.get_barrier_semaphore()
    for k in range(1, nd):
        pl.semaphore_signal(
            barrier, inc=1, device_id={"date": lax.rem(day + k, nd)}, device_id_type=MESH
        )

    @pl.when(has_up)
    def _():
        pl.semaphore_signal(barrier, inc=1, device_id={"tile": tile - 1}, device_id_type=MESH)

    @pl.when(has_down)
    def _():
        pl.semaphore_signal(barrier, inc=1, device_id={"tile": tile + 1}, device_id_type=MESH)

    at_out = lax.broadcasted_iota(jnp.int32, (own, total), 0)
    at_in = lax.broadcasted_iota(jnp.int32, (own, total), 1)
    q = at_out >> 3
    date_out = jnp.where(q < 2, q, jnp.where(q < 4, q - 4 + dates, q - 2))
    row_out = at_out & 7
    date_a, row_a = strip_rows(at_in, dates)
    date_b, row_b = halo_rows(at_in - strip, dates, -2, rows)
    inside = at_in < strip
    apart = jnp.where(inside, date_a, date_b) - date_out
    below = jnp.where(inside, row_a, row_b) - row_out
    weight_t = jnp.zeros((own, total), F32)
    weight_r = jnp.zeros((own, total), F32)
    for k in range(5):
        weight_t = weight_t + jnp.where(apart == k - 2, time_k[k], 0.0)
        weight_r = weight_r + jnp.where(below == k - 2, space_k[k], 0.0)
    weight = weight_t * weight_r
    weight_hi = weight.astype(BF16).astype(F32)
    smooth_m[...] = jnp.concatenate([weight_hi, weight - weight_hi], axis=0).astype(BF16)

    pick = lax.broadcasted_iota(jnp.int32, (2 * PACK, strip), 0)
    date_p, row_p = halo_rows(pick, dates, rows - 2, 0)
    date_s, row_s = strip_rows(lax.broadcasted_iota(jnp.int32, (2 * PACK, strip), 1), dates)
    hit = jnp.logical_and(date_p == date_s, row_p == row_s)
    select_m[...] = jnp.where(hit, 1.0, 0.0).astype(BF16)

    zero_days = jnp.zeros((2 * rows, cols), BF16)
    zero_rows = jnp.zeros((PACK, cols), BF16)

    @pl.loop(0, bands + 1)
    def _(c):
        @pl.when(jnp.logical_not(has_low))
        def _():
            chan[c, pl.ds(0, 2 * rows)] = zero_days

        @pl.when(jnp.logical_not(has_high))
        def _():
            chan[c, pl.ds(2 * rows, 2 * rows)] = zero_days

        @pl.when(jnp.logical_not(has_up))
        def _():
            chan[c, pl.ds(strip, PACK)] = zero_rows

        @pl.when(jnp.logical_not(has_down))
        def _():
            chan[c, pl.ds(strip + PACK, PACK)] = zero_rows

    def later(c):
        return pltpu.make_async_remote_copy(
            src_ref=chan.at[c, pl.ds(6 * rows, 2 * rows)],
            dst_ref=chan.at[c, pl.ds(0, 2 * rows)],
            send_sem=date_send.at[c, 0],
            recv_sem=date_recv.at[c, 0],
            device_id={"date": jnp.minimum(day + 1, nd - 1)},
            device_id_type=MESH,
        )

    def earlier(c):
        return pltpu.make_async_remote_copy(
            src_ref=chan.at[c, pl.ds(4 * rows, 2 * rows)],
            dst_ref=chan.at[c, pl.ds(2 * rows, 2 * rows)],
            send_sem=date_send.at[c, 1],
            recv_sem=date_recv.at[c, 1],
            device_id={"date": jnp.maximum(day - 1, 0)},
            device_id_type=MESH,
        )

    def downward(c):
        return pltpu.make_async_remote_copy(
            src_ref=packed.at[c, pl.ds(0, PACK)],
            dst_ref=chan.at[c, pl.ds(strip, PACK)],
            send_sem=row_send.at[c, 0],
            recv_sem=row_recv.at[c, 0],
            device_id={"tile": jnp.minimum(tile + 1, nt - 1)},
            device_id_type=MESH,
        )

    def upward(c):
        return pltpu.make_async_remote_copy(
            src_ref=packed.at[c, pl.ds(PACK, PACK)],
            dst_ref=chan.at[c, pl.ds(strip + PACK, PACK)],
            send_sem=row_send.at[c, 1],
            recv_sem=row_recv.at[c, 1],
            device_id={"tile": jnp.maximum(tile - 1, 0)},
            device_id_type=MESH,
        )

    def send_dates(c):
        @pl.when(has_high)
        def _():
            later(c).start()

        @pl.when(has_low)
        def _():
            earlier(c).start()

    blank = jnp.zeros((rows, cols), F32)

    def store_own(c, values):
        parts = [values(t) for t in own_order(dates)] + [blank]
        chan[c, pl.ds(4 * rows, own + rows)] = jnp.concatenate(parts, axis=0).astype(BF16)

    mask_in.wait()
    store_own(0, lambda t: cloud[t].astype(F32))
    pl.semaphore_wait(
        barrier, nd - 1 + jnp.where(has_up, 1, 0) + jnp.where(has_down, 1, 0)
    )
    send_dates(0)

    @pl.loop(0, bands)
    def _(b):
        band_in(b).wait()
        store_own(b + 1, lambda t: raw[b, t].astype(F32) * cloud[t].astype(F32))
        send_dates(b + 1)

    def share_rows(c):
        @pl.when(has_low)
        def _():
            later(c).wait_recv()

        @pl.when(has_high)
        def _():
            earlier(c).wait_recv()

        packed[c] = jnp.dot(
            select_m[...], chan[c, pl.ds(0, strip)], preferred_element_type=F32
        ).astype(BF16)

        @pl.when(has_down)
        def _():
            downward(c).start()

        @pl.when(has_up)
        def _():
            upward(c).start()

    def smoothed(c):
        @pl.when(has_up)
        def _():
            downward(c).wait_recv()

        @pl.when(has_down)
        def _():
            upward(c).wait_recv()

        both = jnp.dot(smooth_m[...], chan[c], preferred_element_type=F32)
        rowed = both[:own] + both[own:]
        rowed = jnp.concatenate([rowed, jnp.zeros((own, 128), F32)], axis=1)
        across = cols + 128
        field = space_k[2] * rowed
        for k in (0, 1, 3, 4):
            field = field + space_k[k] * pltpu.roll(rowed, (2 - k) % across, 1)
        return field[:, :cols]

    def own_part(c):
        return chan[c, pl.ds(4 * rows, own + rows)].astype(F32)[:own]

    def send_to(b, k):
        peer = lax.rem(day + k, nd)
        return pltpu.make_async_remote_copy(
            src_ref=out.at[b, peer],
            dst_ref=got.at[b, day],
            send_sem=all_send.at[b],
            recv_sem=all_recv.at[b],
            device_id={"date": peer},
            device_id_type=MESH,
        )

    def fill_out(b):
        return pltpu.make_async_copy(raw.at[b], filled.at[:, b], fill_sem.at[b])

    def coef_out(c):
        return pltpu.make_async_copy(result.at[c], coef.at[c], coef_sem.at[c])

    def fill_band(b):
        whole = own_part(b + 1) + gain[...] * smoothed(b + 1)
        for q, t in enumerate(own_order(dates)):
            strip_t = whole[q * rows : (q + 1) * rows].astype(BF16)
            raw[b, t] = strip_t
            for j in range(nd):
                out[b, j, t] = strip_t[:, j * width : (j + 1) * width]
        for k in range(1, nd):
            send_to(b, (k + nd // 2 - 1) % (nd - 1) + 1).start()
        pltpu.make_async_copy(out.at[b, day], got.at[b, day], all_recv.at[b]).start()
        fill_out(b).start()

    for c in range(AHEAD):
        share_rows(c)
    gain[...] = (1.0 - own_part(0)) / (smoothed(0) + 1.0)

    @pl.loop(0, bands)
    def _(b):
        @pl.when(b + AHEAD <= bands)
        def _():
            share_rows(b + AHEAD)

        fill_band(b)

    fit_copy.wait()

    def project(c, series):
        flat = series.reshape(nd * dates * rows, width).astype(BF16)
        both = jnp.dot(fit[...], flat, preferred_element_type=F32)
        half = TERMS * rows
        result[c] = (both[:half] + both[half:]).reshape(TERMS, rows, width)
        coef_out(c).start()

    def arrived(b):
        pltpu.make_async_copy(got.at[b], got.at[b], all_recv.at[b]).wait()

    @pl.loop(0, bands - 1)
    def _(b):
        arrived(b)
        project(b, got[b].astype(F32))

    red, near, swir = got[2].astype(F32), got[6].astype(F32), got[8].astype(F32)
    project(bands, 1.5 * (near - red) / (near + red + 0.5))
    project(bands + 1, (near - swir) / (near + swir + 0.5))
    arrived(bands - 1)
    project(bands - 1, got[bands - 1].astype(F32))

    @pl.loop(0, bands + 1)
    def _(c):
        @pl.when(has_high)
        def _():
            later(c).wait_send()

        @pl.when(has_low)
        def _():
            earlier(c).wait_send()

        @pl.when(has_down)
        def _():
            downward(c).wait_send()

        @pl.when(has_up)
        def _():
            upward(c).wait_send()

    @pl.loop(0, bands)
    def _(b):
        fill_out(b).wait()
        sent = out.at[b, pl.ds(0, nd - 1)]
        pltpu.make_async_copy(sent, sent, all_send.at[b]).wait()

    @pl.loop(0, bands + 2)
    def _(c):
        coef_out(c).wait()


def solution(mesh):
    nd, nt = mesh.shape["date"], mesh.shape["tile"]

    def per_device(reflectance, clear_mask, time_kernel, space_kernel):
        dates, bands, rows, cols = reflectance.shape
        width = cols // nd
        own = dates * rows
        strip = 4 * rows + own + rows
        total = strip + 2 * PACK
        whole = nd * own
        anywhere = pl.BlockSpec(memory_space=pl.ANY)
        scalars = pl.BlockSpec(memory_space=pltpu.SMEM)
        dma = pltpu.SemaphoreType.DMA
        return pl.pallas_call(
            functools.partial(kernel, (nd, nt, dates, bands, rows, cols)),
            out_shape=(
                jax.ShapeDtypeStruct((dates, bands, rows, cols), BF16),
                jax.ShapeDtypeStruct((bands + 2, TERMS, rows, width), F32),
            ),
            in_specs=[anywhere, anywhere, scalars, scalars, anywhere],
            out_specs=(anywhere, anywhere),
            scratch_shapes=[
                pltpu.VMEM((bands, dates, rows, cols), BF16),
                pltpu.VMEM((dates, rows, cols), jnp.int32),
                pltpu.VMEM((2 * TERMS * rows, whole), BF16),
                pltpu.VMEM((bands + 1, total, cols), BF16),
                pltpu.VMEM((bands + 1, 2 * PACK, cols), BF16),
                pltpu.VMEM((own, cols), F32),
                pltpu.VMEM((bands, nd, dates, rows, width), BF16),
                pltpu.VMEM((bands, nd, dates, rows, width), BF16),
                pltpu.VMEM((bands + 2, TERMS, rows, width), F32),
                pltpu.VMEM((2 * own, total), BF16),
                pltpu.VMEM((2 * PACK, strip), BF16),
                dma((bands + 2,)),
                dma((bands + 1, 2)),
                dma((bands + 1, 2)),
                dma((bands + 1, 2)),
                dma((bands + 1, 2)),
                dma((bands,)),
                dma((bands,)),
                dma((bands,)),
                dma((bands + 2,)),
            ],
            compiler_params=pltpu.CompilerParams(
                collective_id=0, has_side_effects=True, vmem_limit_bytes=56 * 2**20
            ),
            name="fill_and_fit",
        )(
            reflectance,
            clear_mask,
            time_kernel,
            space_kernel,
            jnp.asarray(fit_operand(nd * dates, rows)),
        )

    placed = (P("date", None, "tile", None), P("date", "tile", None), P(), P())
    return jax.shard_map(
        per_device,
        mesh=mesh,
        in_specs=placed,
        out_specs=(P("date", None, "tile", None), P(None, None, "tile", "date")),
        check_vma=False,
    )
```

```python
import functools
import math

import jax
import jax.numpy as jnp
import numpy as np
from jax import lax
from jax.experimental import pallas as pl
from jax.experimental.pallas import tpu as pltpu
from jax.sharding import PartitionSpec as P

TERMS = 24
PACK = 32
AHEAD = 4
MESH = pl.DeviceIdType.MESH
F32 = jnp.float32
BF16 = jnp.bfloat16


def fit_matrix(dates, terms):
    steps = np.arange(dates, dtype=np.float64)
    columns = [np.ones((dates,)), steps / dates - 0.5]
    for order in range(1, (terms - 2) // 2 + 1):
        angle = 2.0 * math.pi * order * steps / dates
        columns.append(np.cos(angle))
        columns.append(np.sin(angle))
    basis = np.stack(columns, axis=1)
    factor = np.linalg.cholesky(basis.T @ basis)
    return np.linalg.solve(factor.T, np.linalg.solve(factor, basis.T))


def fit_operand(dates, rows):
    wide = np.kron(fit_matrix(dates, TERMS), np.eye(rows)).astype(np.float32)
    high = wide.astype(BF16)
    rest = (wide - high.astype(np.float32)).astype(BF16)
    return np.concatenate([high, rest], axis=0)


def own_order(dates):
    return [0, 1, dates - 2, dates - 1] + list(range(2, dates - 2))


def strip_rows(n, dates):
    q = n >> 3
    date = jnp.where(q < 4 + dates, q - 6, -100)
    date = jnp.where(q < 8, q - 8 + dates, date)
    date = jnp.where(q < 6, q - 4, date)
    date = jnp.where(q < 4, q - 2 + dates, date)
    date = jnp.where(q < 2, q - 2, date)
    return date, n & 7


def halo_rows(m, dates, low, high):
    at = m & (PACK - 1)
    date = jnp.where(at < 2 * (dates + 4), (at >> 1) - 2, -200)
    return date, (at & 1) + jnp.where(m < PACK, low, high)


def relay(c, way, half, channels):
    return 2 * (c + 1) + way if half >= 2 * (channels + 2) else 1


def kernel(
    sizes,
    refl, mask, time_k, space_k, fit_in,
    filled, coef,
    raw, cloud, fit, chan, packed, hold, gain, out, got, result, smooth_m, select_m,
    in_sem, date_send, date_recv, row_send, row_recv, hop_send, hop_recv,
    all_send, all_recv, fill_sem, coef_sem,
):
    nd, nt, dates, bands, rows, cols = sizes
    width = cols // nd
    own = dates * rows
    strip = 4 * rows + own + rows
    total = strip + 2 * PACK
    day = lax.axis_index("date")
    tile = lax.axis_index("tile")
    has_low, has_high = day > 0, day < nd - 1
    has_up, has_down = tile > 0, tile < nt - 1
    half = nt // 2
    ends_low, ends_high = tile == half - 1, tile == half
    channels = bands + 1

    def passes(c, way):
        return tile == (half if way else 0) + relay(c, way, half, channels)

    def band_in(b):
        return pltpu.make_async_copy(refl.at[:, b], raw.at[b], in_sem.at[b])

    mask_in = pltpu.make_async_copy(mask, cloud, in_sem.at[bands])
    fit_copy = pltpu.make_async_copy(fit_in, fit, in_sem.at[bands + 1])
    barrier = pltpu.get_barrier_semaphore()
    for k in range(1, nd):
        pl.semaphore_signal(
            barrier, inc=1, device_id={"date": lax.rem(day + k, nd)}, device_id_type=MESH
        )

    def greet(strip):
        pl.semaphore_signal(barrier, inc=1, device_id={"tile": strip}, device_id_type=MESH)

    mask_in.start()

    @pl.loop(0, bands)
    def _(b):
        band_in(b).start()

    fit_copy.start()

    pl.when(has_up)(lambda: greet(tile - 1))
    pl.when(has_down)(lambda: greet(tile + 1))
    greeted = jnp.where(has_up, 1, 0) + jnp.where(has_down, 1, 0)
    greeted = greeted + jnp.where(jnp.logical_or(ends_low, ends_high), bands, 0)

    @pl.loop(1, channels)
    def _(c):
        for way in (0, 1):
            at = (half if way else 0) + relay(c, way, half, channels)
            pl.when(passes(c, way))(lambda: greet(half if way else half - 1))
            pl.when(ends_low if way else ends_high)(lambda: greet(at))

    for way in (0, 1):

        def count(c, total):
            return total + jnp.where(passes(c, way), 1, 0)

        greeted = lax.fori_loop(1, channels, count, greeted)

    def later(c):
        return pltpu.make_async_remote_copy(
            src_ref=chan.at[c, pl.ds(6 * rows, 2 * rows)],
            dst_ref=chan.at[c, pl.ds(0, 2 * rows)],
            send_sem=date_send.at[c, 0],
            recv_sem=date_recv.at[c, 0],
            device_id={"date": jnp.minimum(day + 1, nd - 1)},
            device_id_type=MESH,
        )

    def earlier(c):
        return pltpu.make_async_remote_copy(
            src_ref=chan.at[c, pl.ds(4 * rows, 2 * rows)],
            dst_ref=chan.at[c, pl.ds(2 * rows, 2 * rows)],
            send_sem=date_send.at[c, 1],
            recv_sem=date_recv.at[c, 1],
            device_id={"date": jnp.maximum(day - 1, 0)},
            device_id_type=MESH,
        )

    def downward(c):
        return pltpu.make_async_remote_copy(
            src_ref=packed.at[c, pl.ds(0, PACK)],
            dst_ref=chan.at[c, pl.ds(strip, PACK)],
            send_sem=row_send.at[c, 0],
            recv_sem=row_recv.at[c, 0],
            device_id={"tile": jnp.minimum(tile + 1, nt - 1)},
            device_id_type=MESH,
        )

    def upward(c):
        return pltpu.make_async_remote_copy(
            src_ref=packed.at[c, pl.ds(PACK, PACK)],
            dst_ref=chan.at[c, pl.ds(strip + PACK, PACK)],
            send_sem=row_send.at[c, 1],
            recv_sem=row_recv.at[c, 1],
            device_id={"tile": jnp.maximum(tile - 1, 0)},
            device_id_type=MESH,
        )

    def depart(c, way):
        return pltpu.make_async_remote_copy(
            src_ref=packed.at[c, pl.ds(way * PACK, PACK)],
            dst_ref=hold.at[way, c],
            send_sem=row_send.at[c, way],
            recv_sem=hop_recv.at[way, c],
            device_id={"tile": (half if way else 0) + relay(c, way, half, channels)},
            device_id_type=MESH,
        )

    def arrive(c, way):
        return pltpu.make_async_remote_copy(
            src_ref=hold.at[way, c],
            dst_ref=chan.at[c, pl.ds(strip + way * PACK, PACK)],
            send_sem=hop_send.at[way, c],
            recv_sem=row_recv.at[c, way],
            device_id={"tile": half - 1 if way else half},
            device_id_type=MESH,
        )

    def pass_on(c):
        for way in (0, 1):

            @pl.when(passes(c, way))
            def _():
                depart(c, way).wait_recv()
                arrive(c, way).start()

    def send_dates(c):
        @pl.when(has_high)
        def _():
            later(c).start()

        @pl.when(has_low)
        def _():
            earlier(c).start()

    blank = jnp.zeros((rows, cols), F32)

    def store_own(c, values):
        parts = [values(t) for t in own_order(dates)] + [blank]
        chan[c, pl.ds(4 * rows, own + rows)] = jnp.concatenate(parts, axis=0).astype(BF16)

    mask_in.wait()
    store_own(0, lambda t: cloud[t].astype(F32))
    pl.semaphore_wait(barrier, nd - 1 + greeted)
    send_dates(0)

    @pl.loop(0, bands)
    def _(b):
        band_in(b).wait()
        store_own(b + 1, lambda t: raw[b, t].astype(F32) * cloud[t].astype(F32))
        send_dates(b + 1)

    at_out = lax.broadcasted_iota(jnp.int32, (own, total), 0)
    at_in = lax.broadcasted_iota(jnp.int32, (own, total), 1)
    q = at_out >> 3
    date_out = jnp.where(q < 2, q, jnp.where(q < 4, q - 4 + dates, q - 2))
    row_out = at_out & 7
    date_a, row_a = strip_rows(at_in, dates)
    date_b, row_b = halo_rows(at_in - strip, dates, -2, rows)
    inside = at_in < strip
    apart = jnp.where(inside, date_a, date_b) - date_out
    below = jnp.where(inside, row_a, row_b) - row_out
    weight_t = jnp.zeros((own, total), F32)
    weight_r = jnp.zeros((own, total), F32)
    for k in range(5):
        weight_t = weight_t + jnp.where(apart == k - 2, time_k[k], 0.0)
        weight_r = weight_r + jnp.where(below == k - 2, space_k[k], 0.0)
    weight = weight_t * weight_r
    weight_hi = weight.astype(BF16).astype(F32)
    smooth_m[...] = jnp.concatenate([weight_hi, weight - weight_hi], axis=0).astype(BF16)

    pick = lax.broadcasted_iota(jnp.int32, (2 * PACK, strip), 0)
    date_p, row_p = halo_rows(pick, dates, rows - 2, 0)
    date_s, row_s = strip_rows(lax.broadcasted_iota(jnp.int32, (2 * PACK, strip), 1), dates)
    hit = jnp.logical_and(date_p == date_s, row_p == row_s)
    select_m[...] = jnp.where(hit, 1.0, 0.0).astype(BF16)

    zero_days = jnp.zeros((2 * rows, cols), BF16)
    zero_rows = jnp.zeros((PACK, cols), BF16)

    @pl.loop(0, bands + 1)
    def _(c):
        @pl.when(jnp.logical_not(has_low))
        def _():
            chan[c, pl.ds(0, 2 * rows)] = zero_days

        @pl.when(jnp.logical_not(has_high))
        def _():
            chan[c, pl.ds(2 * rows, 2 * rows)] = zero_days

        @pl.when(jnp.logical_not(has_up))
        def _():
            chan[c, pl.ds(strip, PACK)] = zero_rows

        @pl.when(jnp.logical_not(has_down))
        def _():
            chan[c, pl.ds(strip + PACK, PACK)] = zero_rows

    def share_rows(c):
        @pl.when(has_low)
        def _():
            later(c).wait_recv()

        @pl.when(has_high)
        def _():
            earlier(c).wait_recv()

        packed[c] = jnp.dot(
            select_m[...], chan[c, pl.ds(0, strip)], preferred_element_type=F32
        ).astype(BF16)

        far = c > 0
        by_relay = jnp.logical_and(ends_low, far), jnp.logical_and(ends_high, far)
        pl.when(jnp.logical_and(has_down, jnp.logical_not(by_relay[0])))(lambda: downward(c).start())
        pl.when(jnp.logical_and(has_up, jnp.logical_not(by_relay[1])))(lambda: upward(c).start())
        pl.when(by_relay[0])(lambda: depart(c, 0).start())
        pl.when(by_relay[1])(lambda: depart(c, 1).start())

    def smoothed(c):
        @pl.when(has_up)
        def _():
            downward(c).wait_recv()

        @pl.when(has_down)
        def _():
            upward(c).wait_recv()

        both = jnp.dot(smooth_m[...], chan[c], preferred_element_type=F32)
        rowed = both[:own] + both[own:]
        rowed = jnp.concatenate([rowed, jnp.zeros((own, 128), F32)], axis=1)
        across = cols + 128
        field = space_k[2] * rowed
        for k in (0, 1, 3, 4):
            field = field + space_k[k] * pltpu.roll(rowed, (2 - k) % across, 1)
        return field[:, :cols]

    def own_part(c):
        return chan[c, pl.ds(4 * rows, own + rows)].astype(F32)[:own]

    def send_to(b, k):
        peer = lax.rem(day + k, nd)
        return pltpu.make_async_remote_copy(
            src_ref=out.at[b, peer],
            dst_ref=got.at[b, day],
            send_sem=all_send.at[b],
            recv_sem=all_recv.at[b],
            device_id={"date": peer},
            device_id_type=MESH,
        )

    def fill_out(b):
        return pltpu.make_async_copy(raw.at[b], filled.at[:, b], fill_sem.at[b])

    def coef_out(c):
        return pltpu.make_async_copy(result.at[c], coef.at[c], coef_sem.at[c])

    def fill_band(b):
        whole = own_part(b + 1) + gain[...] * smoothed(b + 1)
        for q, t in enumerate(own_order(dates)):
            strip_t = whole[q * rows : (q + 1) * rows].astype(BF16)
            raw[b, t] = strip_t
            for j in range(nd):
                out[b, j, t] = strip_t[:, j * width : (j + 1) * width]
        for k in sorted(range(1, nd), key=lambda k: abs(2 * k - nd)):
            send_to(b, k).start()
        pltpu.make_async_copy(out.at[b, day], got.at[b, day], all_recv.at[b]).start()
        fill_out(b).start()

    for c in range(AHEAD):
        share_rows(c)
        if c >= 2:
            pass_on(c - 1)

    gain[...] = (1.0 - own_part(0)) / (smoothed(0) + 1.0)

    @pl.loop(0, bands)
    def _(b):
        @pl.when(b + AHEAD <= bands)
        def _():
            share_rows(b + AHEAD)

        @pl.when(b + AHEAD - 1 <= bands)
        def _():
            pass_on(b + AHEAD - 1)

        fill_band(b)

    fit_copy.wait()

    def project(c, series):
        flat = series.reshape(nd * dates * rows, width).astype(BF16)
        both = jnp.dot(fit[...], flat, preferred_element_type=F32)
        half = TERMS * rows
        result[c] = (both[:half] + both[half:]).reshape(TERMS, rows, width)
        coef_out(c).start()

    def arrived(b):
        pltpu.make_async_copy(got.at[b], got.at[b], all_recv.at[b]).wait()

    @pl.loop(0, bands - 1)
    def _(b):
        arrived(b)
        project(b, got[b].astype(F32))

    red, near, swir = got[2].astype(F32), got[6].astype(F32), got[8].astype(F32)
    project(bands, 1.5 * (near - red) / (near + red + 0.5))
    project(bands + 1, (near - swir) / (near + swir + 0.5))
    arrived(bands - 1)
    project(bands - 1, got[bands - 1].astype(F32))

    @pl.loop(0, bands + 1)
    def _(c):
        @pl.when(has_high)
        def _():
            later(c).wait_send()

        @pl.when(has_low)
        def _():
            earlier(c).wait_send()

        pl.when(has_down)(lambda: downward(c).wait_send())
        pl.when(has_up)(lambda: upward(c).wait_send())

    @pl.loop(1, channels)
    def _(c):
        for way in (0, 1):
            pl.when(passes(c, way))(lambda: arrive(c, way).wait_send())

    @pl.loop(0, bands)
    def _(b):
        fill_out(b).wait()
        sent = out.at[b, pl.ds(0, nd - 1)]
        pltpu.make_async_copy(sent, sent, all_send.at[b]).wait()

    @pl.loop(0, bands + 2)
    def _(c):
        coef_out(c).wait()


def hand_over(filled_in, coef_in, filled, coef, fill_at, coef_at, fill_sem, coef_sem):
    steps = []
    for source, at, target, sem in (
        (filled_in, fill_at, filled, fill_sem),
        (coef_in, coef_at, coef, coef_sem),
    ):
        size = source.shape[0] // 3
        steps += [(source, at, target, sem, i, pl.ds(i * size, size)) for i in range(3)]

    def load(source, at, _, sem, i, part):
        return pltpu.make_async_copy(source.at[part], at.at[part], sem.at[0, i])

    def store(_, at, target, sem, i, part):
        return pltpu.make_async_copy(at.at[part], target.at[part], sem.at[1, i])

    for step in steps:
        load(*step).start()
    for step in steps:
        load(*step).wait()
        store(*step).start()
    for step in steps:
        store(*step).wait()


def solution(mesh):
    nd, nt = mesh.shape["date"], mesh.shape["tile"]

    def per_device(reflectance, clear_mask, time_kernel, space_kernel):
        dates, bands, rows, cols = reflectance.shape
        width = cols // nd
        own = dates * rows
        strip = 4 * rows + own + rows
        total = strip + 2 * PACK
        whole = nd * own
        anywhere = pl.BlockSpec(memory_space=pl.ANY)
        scalars = pl.BlockSpec(memory_space=pltpu.SMEM)
        dma = pltpu.SemaphoreType.DMA
        shapes = (
            jax.ShapeDtypeStruct((dates, bands, rows, cols), BF16),
            jax.ShapeDtypeStruct((bands + 2, TERMS, rows, width), F32),
        )
        results = pl.pallas_call(
            functools.partial(kernel, (nd, nt, dates, bands, rows, cols)),
            out_shape=shapes,
            in_specs=[anywhere, anywhere, scalars, scalars, anywhere],
            out_specs=(anywhere, anywhere),
            scratch_shapes=[
                pltpu.VMEM((bands, dates, rows, cols), BF16),
                pltpu.VMEM((dates, rows, cols), jnp.int32),
                pltpu.VMEM((2 * TERMS * rows, whole), BF16),
                pltpu.VMEM((bands + 1, total, cols), BF16),
                pltpu.VMEM((bands + 1, 2 * PACK, cols), BF16),
                pltpu.VMEM((2, bands + 1, PACK, cols), BF16),
                pltpu.VMEM((own, cols), F32),
                pltpu.VMEM((bands, nd, dates, rows, width), BF16),
                pltpu.VMEM((bands, nd, dates, rows, width), BF16),
                pltpu.VMEM((bands + 2, TERMS, rows, width), F32),
                pltpu.VMEM((2 * own, total), BF16),
                pltpu.VMEM((2 * PACK, strip), BF16),
                dma((bands + 2,)),
                dma((bands + 1, 2)),
                dma((bands + 1, 2)),
                dma((bands + 1, 2)),
                dma((bands + 1, 2)),
                dma((2, bands + 1)),
                dma((2, bands + 1)),
                dma((bands,)),
                dma((bands,)),
                dma((bands,)),
                dma((bands + 2,)),
            ],
            compiler_params=pltpu.CompilerParams(
                collective_id=0, has_side_effects=True, vmem_limit_bytes=56 * 2**20
            ),
            name="fill_and_fit",
        )(
            reflectance,
            clear_mask,
            time_kernel,
            space_kernel,
            jnp.asarray(fit_operand(nd * dates, rows)),
        )
        return pl.pallas_call(
            hand_over,
            out_shape=shapes,
            in_specs=[anywhere, anywhere],
            out_specs=(anywhere, anywhere),
            scratch_shapes=[
                pltpu.VMEM((dates, bands, rows, cols), BF16),
                pltpu.VMEM((bands + 2, TERMS, rows, width), F32),
                dma((2, 3)),
                dma((2, 3)),
            ],
            compiler_params=pltpu.CompilerParams(vmem_limit_bytes=60 * 2**20),
            name="hand_over",
        )(*results)

    placed = (P("date", None, "tile", None), P("date", "tile", None), P(), P())
    return jax.shard_map(
        per_device,
        mesh=mesh,
        in_specs=placed,
        out_specs=(P("date", None, "tile", None), P(None, None, "tile", "date")),
        check_vma=False,
    )
```

```python
import functools
import math

import jax
import jax.numpy as jnp
import numpy as np
from jax import lax
from jax.experimental import pallas as pl
from jax.experimental.pallas import tpu as pltpu
from jax.sharding import PartitionSpec as P

TERMS = 24
PACK = 32
AHEAD = 4
MESH = pl.DeviceIdType.MESH
F32 = jnp.float32
BF16 = jnp.bfloat16


def fit_matrix(dates, terms):
    steps = np.arange(dates, dtype=np.float64)
    columns = [np.ones((dates,)), steps / dates - 0.5]
    for order in range(1, (terms - 2) // 2 + 1):
        angle = 2.0 * math.pi * order * steps / dates
        columns.append(np.cos(angle))
        columns.append(np.sin(angle))
    basis = np.stack(columns, axis=1)
    factor = np.linalg.cholesky(basis.T @ basis)
    return np.linalg.solve(factor.T, np.linalg.solve(factor, basis.T))


def fit_operand(dates, rows):
    wide = np.kron(fit_matrix(dates, TERMS), np.eye(rows)).astype(np.float32)
    high = wide.astype(BF16)
    rest = (wide - high.astype(np.float32)).astype(BF16)
    return np.concatenate([high, rest], axis=0)


def own_order(dates):
    return [0, 1, dates - 2, dates - 1] + list(range(2, dates - 2))


def strip_rows(n, dates):
    q = n >> 3
    date = jnp.where(q < 4 + dates, q - 6, -100)
    date = jnp.where(q < 8, q - 8 + dates, date)
    date = jnp.where(q < 6, q - 4, date)
    date = jnp.where(q < 4, q - 2 + dates, date)
    date = jnp.where(q < 2, q - 2, date)
    return date, n & 7


def halo_rows(m, dates, low, high):
    at = m & (PACK - 1)
    date = jnp.where(at < 2 * (dates + 4), (at >> 1) - 2, -200)
    return date, (at & 1) + jnp.where(m < PACK, low, high)


def relay(c, way, half, channels):
    return 2 * (c + 1) + way if half >= 2 * (channels + 2) else 1


def kernel(
    sizes,
    refl, mask, time_k, space_k, fit_in,
    filled, coef,
    raw, cloud, fit, chan, packed, hold, gain, out, got, smooth_m, select_m,
    in_sem, date_send, date_recv, row_send, row_recv, hop_send, hop_recv,
    all_send, all_recv, ready,
):
    nd, nt, dates, bands, rows, cols = sizes
    width = cols // nd
    own = dates * rows
    strip = 4 * rows + own + rows
    total = strip + 2 * PACK
    day = lax.axis_index("date")
    tile = lax.axis_index("tile")
    has_low, has_high = day > 0, day < nd - 1
    has_up, has_down = tile > 0, tile < nt - 1
    half = nt // 2
    ends_low, ends_high = tile == half - 1, tile == half
    channels = bands + 1

    def passes(c, way):
        return tile == (half if way else 0) + relay(c, way, half, channels)

    def band_in(b):
        return pltpu.make_async_copy(refl.at[:, b], raw.at[b], in_sem.at[b])

    mask_in = pltpu.make_async_copy(mask, cloud, in_sem.at[bands])
    fit_copy = pltpu.make_async_copy(fit_in, fit, in_sem.at[bands + 1])
    barrier = pltpu.get_barrier_semaphore()
    for k in range(1, nd):
        pl.semaphore_signal(
            barrier, inc=1, device_id={"date": lax.rem(day + k, nd)}, device_id_type=MESH
        )

    def greet(strip):
        pl.semaphore_signal(barrier, inc=1, device_id={"tile": strip}, device_id_type=MESH)

    mask_in.start()

    @pl.loop(0, bands)
    def _(b):
        band_in(b).start()

    fit_copy.start()

    pl.when(jnp.logical_and(has_up, tile != half))(lambda: greet(tile - 1))
    pl.when(has_down)(lambda: greet(tile + 1))
    greeted = jnp.where(has_up, 1, 0)
    greeted = greeted + jnp.where(jnp.logical_and(has_down, tile != half - 1), 1, 0)
    greeted = greeted + jnp.where(ends_low, bands, 0) + jnp.where(ends_high, 2 * bands, 0)

    @pl.loop(1, channels)
    def _(c):
        @pl.when(passes(c, 0))
        def _():
            greet(half - 1)
            greet(half)

        pl.when(passes(c, 1))(lambda: greet(half))
        pl.when(ends_low)(lambda: greet(half + relay(c, 1, half, channels)))

    def count(c, total):
        return total + jnp.where(passes(c, 1), 1, 0)

    greeted = lax.fori_loop(1, channels, count, greeted)

    def tell_ready(strip):
        pl.semaphore_signal(ready, inc=1, device_id={"tile": strip}, device_id_type=MESH)

    def later(c):
        return pltpu.make_async_remote_copy(
            src_ref=chan.at[c, pl.ds(6 * rows, 2 * rows)],
            dst_ref=chan.at[c, pl.ds(0, 2 * rows)],
            send_sem=date_send.at[c, 0],
            recv_sem=date_recv.at[c, 0],
            device_id={"date": jnp.minimum(day + 1, nd - 1)},
            device_id_type=MESH,
        )

    def earlier(c):
        return pltpu.make_async_remote_copy(
            src_ref=chan.at[c, pl.ds(4 * rows, 2 * rows)],
            dst_ref=chan.at[c, pl.ds(2 * rows, 2 * rows)],
            send_sem=date_send.at[c, 1],
            recv_sem=date_recv.at[c, 1],
            device_id={"date": jnp.maximum(day - 1, 0)},
            device_id_type=MESH,
        )

    def downward(c):
        return pltpu.make_async_remote_copy(
            src_ref=packed.at[c, pl.ds(0, PACK)],
            dst_ref=chan.at[c, pl.ds(strip, PACK)],
            send_sem=row_send.at[c, 0],
            recv_sem=row_recv.at[c, 0],
            device_id={"tile": jnp.minimum(tile + 1, nt - 1)},
            device_id_type=MESH,
        )

    def upward(c):
        return pltpu.make_async_remote_copy(
            src_ref=packed.at[c, pl.ds(PACK, PACK)],
            dst_ref=chan.at[c, pl.ds(strip + PACK, PACK)],
            send_sem=row_send.at[c, 1],
            recv_sem=row_recv.at[c, 1],
            device_id={"tile": jnp.maximum(tile - 1, 0)},
            device_id_type=MESH,
        )

    def depart(c, way):
        return pltpu.make_async_remote_copy(
            src_ref=packed.at[c, pl.ds(way * PACK, PACK)],
            dst_ref=hold.at[way, c],
            send_sem=row_send.at[c, way],
            recv_sem=hop_recv.at[way, c],
            device_id={"tile": (half if way else 0) + relay(c, way, half, channels)},
            device_id_type=MESH,
        )

    def arrive(c, way):
        return pltpu.make_async_remote_copy(
            src_ref=hold.at[way, c],
            dst_ref=chan.at[c, pl.ds(strip + way * PACK, PACK)],
            send_sem=hop_send.at[way, c],
            recv_sem=row_recv.at[c, way],
            device_id={"tile": half - 1 if way else half},
            device_id_type=MESH,
        )

    def pass_on(c, way):
        @pl.when(passes(c, way))
        def _():
            depart(c, way).wait_recv()
            if way == 0:
                pl.semaphore_wait(ready, 1)
            arrive(c, way).start()

    def send_dates(c):
        @pl.when(has_high)
        def _():
            later(c).start()

        @pl.when(has_low)
        def _():
            earlier(c).start()

    blank = jnp.zeros((rows, cols), F32)

    def store_own(c, values):
        parts = [values(t) for t in own_order(dates)] + [blank]
        chan[c, pl.ds(4 * rows, own + rows)] = jnp.concatenate(parts, axis=0).astype(BF16)

    mask_in.wait()
    store_own(0, lambda t: cloud[t].astype(F32))
    pl.semaphore_wait(barrier, nd - 1 + greeted)

    @pl.when(ends_high)
    def _():
        tell_ready(half - 1)

        @pl.loop(1, channels)
        def _(c):
            tell_ready(relay(c, 0, half, channels))

    send_dates(0)

    @pl.loop(0, bands)
    def _(b):
        band_in(b).wait()
        store_own(b + 1, lambda t: raw[b, t].astype(F32) * cloud[t].astype(F32))
        send_dates(b + 1)

    at_out = lax.broadcasted_iota(jnp.int32, (own, total), 0)
    at_in = lax.broadcasted_iota(jnp.int32, (own, total), 1)
    q = at_out >> 3
    date_out = jnp.where(q < 2, q, jnp.where(q < 4, q - 4 + dates, q - 2))
    row_out = at_out & 7
    date_a, row_a = strip_rows(at_in, dates)
    date_b, row_b = halo_rows(at_in - strip, dates, -2, rows)
    inside = at_in < strip
    apart = jnp.where(inside, date_a, date_b) - date_out
    below = jnp.where(inside, row_a, row_b) - row_out
    weight_t = jnp.zeros((own, total), F32)
    weight_r = jnp.zeros((own, total), F32)
    for k in range(5):
        weight_t = weight_t + jnp.where(apart == k - 2, time_k[k], 0.0)
        weight_r = weight_r + jnp.where(below == k - 2, space_k[k], 0.0)
    weight = weight_t * weight_r
    weight_hi = weight.astype(BF16).astype(F32)
    smooth_m[...] = jnp.concatenate([weight_hi, weight - weight_hi], axis=0).astype(BF16)

    pick = lax.broadcasted_iota(jnp.int32, (2 * PACK, strip), 0)
    date_p, row_p = halo_rows(pick, dates, rows - 2, 0)
    date_s, row_s = strip_rows(lax.broadcasted_iota(jnp.int32, (2 * PACK, strip), 1), dates)
    hit = jnp.logical_and(date_p == date_s, row_p == row_s)
    select_m[...] = jnp.where(hit, 1.0, 0.0).astype(BF16)

    zero_days = jnp.zeros((2 * rows, cols), BF16)
    zero_rows = jnp.zeros((PACK, cols), BF16)

    @pl.loop(0, bands + 1)
    def _(c):
        @pl.when(jnp.logical_not(has_low))
        def _():
            chan[c, pl.ds(0, 2 * rows)] = zero_days

        @pl.when(jnp.logical_not(has_high))
        def _():
            chan[c, pl.ds(2 * rows, 2 * rows)] = zero_days

        @pl.when(jnp.logical_not(has_up))
        def _():
            chan[c, pl.ds(strip, PACK)] = zero_rows

        @pl.when(jnp.logical_not(has_down))
        def _():
            chan[c, pl.ds(strip + PACK, PACK)] = zero_rows

    def share_rows(c):
        @pl.when(has_low)
        def _():
            later(c).wait_recv()

        @pl.when(has_high)
        def _():
            earlier(c).wait_recv()

        packed[c] = jnp.dot(
            select_m[...], chan[c, pl.ds(0, strip)], preferred_element_type=F32
        ).astype(BF16)

        far = c > 0
        pl.when(jnp.logical_and(ends_low, c == 0))(lambda: pl.semaphore_wait(ready, 1))
        by_relay = jnp.logical_and(ends_low, far), jnp.logical_and(ends_high, far)
        pl.when(jnp.logical_and(has_down, jnp.logical_not(by_relay[0])))(lambda: downward(c).start())
        pl.when(jnp.logical_and(has_up, jnp.logical_not(by_relay[1])))(lambda: upward(c).start())
        pl.when(by_relay[0])(lambda: depart(c, 0).start())
        pl.when(by_relay[1])(lambda: depart(c, 1).start())

    def smoothed(c):
        @pl.when(has_up)
        def _():
            downward(c).wait_recv()

        @pl.when(has_down)
        def _():
            upward(c).wait_recv()

        both = jnp.dot(smooth_m[...], chan[c], preferred_element_type=F32)
        rowed = both[:own] + both[own:]
        rowed = jnp.concatenate([rowed, jnp.zeros((own, 128), F32)], axis=1)
        across = cols + 128
        field = space_k[2] * rowed
        for k in (0, 1, 3, 4):
            field = field + space_k[k] * pltpu.roll(rowed, (2 - k) % across, 1)
        return field[:, :cols]

    def own_part(c):
        return chan[c, pl.ds(4 * rows, own + rows)].astype(F32)[:own]

    def send_to(b, k):
        peer = lax.rem(day + k, nd)
        return pltpu.make_async_remote_copy(
            src_ref=out.at[b, peer],
            dst_ref=got.at[b, day],
            send_sem=all_send.at[b],
            recv_sem=all_recv.at[b],
            device_id={"date": peer},
            device_id_type=MESH,
        )

    def fill_band(b):
        whole = own_part(b + 1) + gain[...] * smoothed(b + 1)
        for q, t in enumerate(own_order(dates)):
            strip_t = whole[q * rows : (q + 1) * rows].astype(BF16)
            filled[t, b] = strip_t
            for j in range(nd):
                out[b, j, t] = strip_t[:, j * width : (j + 1) * width]
        for k in (4, 3, 5):
            send_to(b, k).start()
        pltpu.make_async_copy(out.at[b, day], got.at[b, day], all_recv.at[b]).start()

    for c in range(AHEAD):
        share_rows(c)
        if c >= 2:
            pass_on(c - 1, 1)

    pass_on(AHEAD - 1, 1)
    pass_on(AHEAD, 1)

    at_gap = jnp.logical_or(ends_low, ends_high)

    @pl.when(at_gap)
    def _():
        @pl.loop(AHEAD, channels)
        def _(c):
            share_rows(c)

    gain[...] = (1.0 - own_part(0)) / (smoothed(0) + 1.0)

    @pl.loop(0, bands)
    def _(b):
        @pl.when(jnp.logical_and(b + AHEAD <= bands, jnp.logical_not(at_gap)))
        def _():
            share_rows(b + AHEAD)

        pl.when(b + AHEAD + 1 <= bands)(lambda: pass_on(b + AHEAD + 1, 1))
        fill_band(b)

        @pl.when(b < 3)
        def _():
            pass_on(2 * b + 1, 0)
            pass_on(2 * b + 2, 0)

        pl.when(jnp.logical_and(b >= 3, b + 4 <= bands))(lambda: pass_on(b + 4, 0))

    for k in (2, 1, 6, 7):
        @pl.loop(0, bands)
        def _(b):
            send_to(b, k).start()

    fit_copy.wait()

    def project(places, pair):
        flat = [x.reshape(nd * dates * rows, width).astype(BF16) for x in pair]
        both = jnp.dot(fit[...], jnp.concatenate(flat, axis=1), preferred_element_type=F32)
        middle = TERMS * rows
        terms = both[:middle] + both[middle:]
        for i, c in enumerate(places):
            coef[c] = terms[:, i * width : (i + 1) * width].reshape(TERMS, rows, width)

    def arrived(b):
        pltpu.make_async_copy(got.at[b], got.at[b], all_recv.at[b]).wait()

    def series(b):
        return got[b].astype(F32)

    @pl.loop(0, bands // 2 - 1)
    def _(i):
        arrived(2 * i)
        arrived(2 * i + 1)
        project((2 * i, 2 * i + 1), (series(2 * i), series(2 * i + 1)))

    arrived(bands - 2)
    red, near, swir = series(2), series(6), series(8)
    savi = 1.5 * (near - red) / (near + red + 0.5)
    project((bands, bands + 1), (savi, (near - swir) / (near + swir + 0.5)))
    arrived(bands - 1)
    project((bands - 2, bands - 1), (series(bands - 2), series(bands - 1)))

    @pl.loop(0, bands + 1)
    def _(c):
        @pl.when(has_high)
        def _():
            later(c).wait_send()

        @pl.when(has_low)
        def _():
            earlier(c).wait_send()

        pl.when(has_down)(lambda: downward(c).wait_send())
        pl.when(has_up)(lambda: upward(c).wait_send())

    @pl.loop(1, channels)
    def _(c):
        for way in (0, 1):
            pl.when(passes(c, way))(lambda: arrive(c, way).wait_send())

    @pl.loop(0, bands)
    def _(b):
        sent = out.at[b, pl.ds(0, nd - 1)]
        pltpu.make_async_copy(sent, sent, all_send.at[b]).wait()


def solution(mesh):
    nd, nt = mesh.shape["date"], mesh.shape["tile"]

    def per_device(reflectance, clear_mask, time_kernel, space_kernel):
        dates, bands, rows, cols = reflectance.shape
        width = cols // nd
        own = dates * rows
        strip = 4 * rows + own + rows
        total = strip + 2 * PACK
        whole = nd * own
        anywhere = pl.BlockSpec(memory_space=pl.ANY)
        inside = pl.BlockSpec(memory_space=pltpu.VMEM)
        scalars = pl.BlockSpec(memory_space=pltpu.SMEM)
        dma = pltpu.SemaphoreType.DMA
        shapes = (
            jax.ShapeDtypeStruct((dates, bands, rows, cols), BF16),
            jax.ShapeDtypeStruct((bands + 2, TERMS, rows, width), F32),
        )
        return pl.pallas_call(
            functools.partial(kernel, (nd, nt, dates, bands, rows, cols)),
            out_shape=tuple(pltpu.VMEM(s.shape, s.dtype) for s in shapes),
            in_specs=[anywhere, anywhere, scalars, scalars, anywhere],
            out_specs=(inside, inside),
            scratch_shapes=[
                pltpu.VMEM((bands, dates, rows, cols), BF16),
                pltpu.VMEM((dates, rows, cols), jnp.int32),
                pltpu.VMEM((2 * TERMS * rows, whole), BF16),
                pltpu.VMEM((bands + 1, total, cols), BF16),
                pltpu.VMEM((bands + 1, 2 * PACK, cols), BF16),
                pltpu.VMEM((2, bands + 1, PACK, cols), BF16),
                pltpu.VMEM((own, cols), F32),
                pltpu.VMEM((bands, nd, dates, rows, width), BF16),
                pltpu.VMEM((bands, nd, dates, rows, width), BF16),
                pltpu.VMEM((2 * own, total), BF16),
                pltpu.VMEM((2 * PACK, strip), BF16),
                dma((bands + 2,)),
                dma((bands + 1, 2)),
                dma((bands + 1, 2)),
                dma((bands + 1, 2)),
                dma((bands + 1, 2)),
                dma((2, bands + 1)),
                dma((2, bands + 1)),
                dma((bands,)),
                dma((bands,)),
                pltpu.SemaphoreType.REGULAR,
            ],
            compiler_params=pltpu.CompilerParams(
                collective_id=0, has_side_effects=True, vmem_limit_bytes=56 * 2**20
            ),
            name="fill_and_fit",
        )(
            reflectance,
            clear_mask,
            time_kernel,
            space_kernel,
            jnp.asarray(fit_operand(nd * dates, rows)),
        )

    placed = (P("date", None, "tile", None), P("date", "tile", None), P(), P())
    return jax.shard_map(
        per_device,
        mesh=mesh,
        in_specs=placed,
        out_specs=(P("date", None, "tile", None), P(None, None, "tile", "date")),
        check_vma=False,
    )
```

```python
import functools
import math

import jax
import jax.numpy as jnp
import numpy as np
from jax import lax
from jax.experimental import pallas as pl
from jax.experimental.pallas import tpu as pltpu
from jax.sharding import PartitionSpec as P

TERMS = 24
PACK = 32
AHEAD = 4
MESH = pl.DeviceIdType.MESH
F32 = jnp.float32
BF16 = jnp.bfloat16


def fit_matrix(dates, terms):
    steps = np.arange(dates, dtype=np.float64)
    columns = [np.ones((dates,)), steps / dates - 0.5]
    for order in range(1, (terms - 2) // 2 + 1):
        angle = 2.0 * math.pi * order * steps / dates
        columns.append(np.cos(angle))
        columns.append(np.sin(angle))
    basis = np.stack(columns, axis=1)
    factor = np.linalg.cholesky(basis.T @ basis)
    return np.linalg.solve(factor.T, np.linalg.solve(factor, basis.T))


def fit_operand(dates, rows):
    wide = np.kron(fit_matrix(dates, TERMS), np.eye(rows)).astype(np.float32)
    high = wide.astype(BF16)
    rest = (wide - high.astype(np.float32)).astype(BF16)
    return np.concatenate([high, rest], axis=0)


def own_order(dates):
    return [0, 1, dates - 2, dates - 1] + list(range(2, dates - 2))


def strip_rows(n, dates):
    q = n >> 3
    date = jnp.where(q < 4 + dates, q - 6, -100)
    date = jnp.where(q < 8, q - 8 + dates, date)
    date = jnp.where(q < 6, q - 4, date)
    date = jnp.where(q < 4, q - 2 + dates, date)
    date = jnp.where(q < 2, q - 2, date)
    return date, n & 7


def halo_rows(m, dates, low, high):
    at = m & (PACK - 1)
    date = jnp.where(at < 2 * (dates + 4), (at >> 1) - 2, -200)
    return date, (at & 1) + jnp.where(m < PACK, low, high)


def relay(c, way, half, channels):
    return 2 * (c + 1) + way if half >= 2 * (channels + 2) else 1


def kernel(
    sizes,
    refl, mask, time_k, space_k, fit_in,
    filled, coef,
    raw, cloud, fit, chan, packed, hold, gain, out, got, smooth_m, select_m,
    in_sem, date_send, date_recv, row_send, row_recv, hop_send, hop_recv,
    all_send, all_recv, ready,
):
    nd, nt, dates, bands, rows, cols = sizes
    width = cols // nd
    own = dates * rows
    strip = 4 * rows + own + rows
    total = strip + 2 * PACK
    day = lax.axis_index("date")
    tile = lax.axis_index("tile")
    has_low, has_high = day > 0, day < nd - 1
    has_up, has_down = tile > 0, tile < nt - 1
    half = nt // 2
    ends_low, ends_high = tile == half - 1, tile == half
    channels = bands + 1

    def passes(c, way):
        return tile == (half if way else 0) + relay(c, way, half, channels)

    def band_in(b):
        return pltpu.make_async_copy(refl.at[:, b], raw.at[b], in_sem.at[b])

    mask_in = pltpu.make_async_copy(mask, cloud, in_sem.at[bands])
    fit_copy = pltpu.make_async_copy(fit_in, fit, in_sem.at[bands + 1])
    barrier = pltpu.get_barrier_semaphore()
    for k in range(1, nd):
        pl.semaphore_signal(
            barrier, inc=1, device_id={"date": lax.rem(day + k, nd)}, device_id_type=MESH
        )

    def greet(strip):
        pl.semaphore_signal(barrier, inc=1, device_id={"tile": strip}, device_id_type=MESH)

    mask_in.start()

    @pl.loop(0, bands)
    def _(b):
        band_in(b).start()

    fit_copy.start()

    pl.when(jnp.logical_and(has_up, tile != half))(lambda: greet(tile - 1))
    pl.when(has_down)(lambda: greet(tile + 1))
    greeted = jnp.where(has_up, 1, 0)
    greeted = greeted + jnp.where(jnp.logical_and(has_down, tile != half - 1), 1, 0)
    greeted = greeted + jnp.where(ends_low, bands, 0) + jnp.where(ends_high, 2 * bands, 0)

    @pl.loop(1, channels)
    def _(c):
        @pl.when(passes(c, 0))
        def _():
            greet(half - 1)
            greet(half)

        pl.when(passes(c, 1))(lambda: greet(half))
        pl.when(ends_low)(lambda: greet(half + relay(c, 1, half, channels)))

    def count(c, total):
        return total + jnp.where(passes(c, 1), 1, 0)

    greeted = lax.fori_loop(1, channels, count, greeted)

    def tell_ready(strip):
        pl.semaphore_signal(ready, inc=1, device_id={"tile": strip}, device_id_type=MESH)

    def later(c):
        return pltpu.make_async_remote_copy(
            src_ref=chan.at[c, pl.ds(6 * rows, 2 * rows)],
            dst_ref=chan.at[c, pl.ds(0, 2 * rows)],
            send_sem=date_send.at[c, 0],
            recv_sem=date_recv.at[c, 0],
            device_id={"date": jnp.minimum(day + 1, nd - 1)},
            device_id_type=MESH,
        )

    def earlier(c):
        return pltpu.make_async_remote_copy(
            src_ref=chan.at[c, pl.ds(4 * rows, 2 * rows)],
            dst_ref=chan.at[c, pl.ds(2 * rows, 2 * rows)],
            send_sem=date_send.at[c, 1],
            recv_sem=date_recv.at[c, 1],
            device_id={"date": jnp.maximum(day - 1, 0)},
            device_id_type=MESH,
        )

    def downward(c):
        return pltpu.make_async_remote_copy(
            src_ref=packed.at[c, pl.ds(0, PACK)],
            dst_ref=chan.at[c, pl.ds(strip, PACK)],
            send_sem=row_send.at[c, 0],
            recv_sem=row_recv.at[c, 0],
            device_id={"tile": jnp.minimum(tile + 1, nt - 1)},
            device_id_type=MESH,
        )

    def upward(c):
        return pltpu.make_async_remote_copy(
            src_ref=packed.at[c, pl.ds(PACK, PACK)],
            dst_ref=chan.at[c, pl.ds(strip + PACK, PACK)],
            send_sem=row_send.at[c, 1],
            recv_sem=row_recv.at[c, 1],
            device_id={"tile": jnp.maximum(tile - 1, 0)},
            device_id_type=MESH,
        )

    def depart(c, way):
        return pltpu.make_async_remote_copy(
            src_ref=packed.at[c, pl.ds(way * PACK, PACK)],
            dst_ref=hold.at[way, c],
            send_sem=row_send.at[c, way],
            recv_sem=hop_recv.at[way, c],
            device_id={"tile": (half if way else 0) + relay(c, way, half, channels)},
            device_id_type=MESH,
        )

    def arrive(c, way):
        return pltpu.make_async_remote_copy(
            src_ref=hold.at[way, c],
            dst_ref=chan.at[c, pl.ds(strip + way * PACK, PACK)],
            send_sem=hop_send.at[way, c],
            recv_sem=row_recv.at[c, way],
            device_id={"tile": half - 1 if way else half},
            device_id_type=MESH,
        )

    def pass_on(c, way):
        @pl.when(passes(c, way))
        def _():
            depart(c, way).wait_recv()
            if way == 0:
                pl.semaphore_wait(ready, 1)
            arrive(c, way).start()

    def send_dates(c):
        @pl.when(has_high)
        def _():
            later(c).start()

        @pl.when(has_low)
        def _():
            earlier(c).start()

    blank = jnp.zeros((rows, cols), F32)

    def store_own(c, values):
        parts = [values(t) for t in own_order(dates)] + [blank]
        chan[c, pl.ds(4 * rows, own + rows)] = jnp.concatenate(parts, axis=0).astype(BF16)

    mask_in.wait()
    store_own(0, lambda t: cloud[t].astype(F32))
    pl.semaphore_wait(barrier, nd - 1 + greeted)

    @pl.when(ends_high)
    def _():
        tell_ready(half - 1)

        @pl.loop(1, channels)
        def _(c):
            tell_ready(relay(c, 0, half, channels))

    send_dates(0)

    @pl.loop(0, bands)
    def _(b):
        band_in(b).wait()
        store_own(b + 1, lambda t: raw[b, t].astype(F32) * cloud[t].astype(F32))
        send_dates(b + 1)

    at_out = lax.broadcasted_iota(jnp.int32, (own, total), 0)
    at_in = lax.broadcasted_iota(jnp.int32, (own, total), 1)
    q = at_out >> 3
    date_out = jnp.where(q < 2, q, jnp.where(q < 4, q - 4 + dates, q - 2))
    row_out = at_out & 7
    date_a, row_a = strip_rows(at_in, dates)
    date_b, row_b = halo_rows(at_in - strip, dates, -2, rows)
    inside = at_in < strip
    apart = jnp.where(inside, date_a, date_b) - date_out
    below = jnp.where(inside, row_a, row_b) - row_out
    weight_t = jnp.zeros((own, total), F32)
    weight_r = jnp.zeros((own, total), F32)
    for k in range(5):
        weight_t = weight_t + jnp.where(apart == k - 2, time_k[k], 0.0)
        weight_r = weight_r + jnp.where(below == k - 2, space_k[k], 0.0)
    weight = weight_t * weight_r
    weight_hi = weight.astype(BF16).astype(F32)
    smooth_m[...] = jnp.concatenate([weight_hi, weight - weight_hi], axis=0).astype(BF16)

    pick = lax.broadcasted_iota(jnp.int32, (2 * PACK, strip), 0)
    date_p, row_p = halo_rows(pick, dates, rows - 2, 0)
    date_s, row_s = strip_rows(lax.broadcasted_iota(jnp.int32, (2 * PACK, strip), 1), dates)
    hit = jnp.logical_and(date_p == date_s, row_p == row_s)
    select_m[...] = jnp.where(hit, 1.0, 0.0).astype(BF16)

    zero_days = jnp.zeros((2 * rows, cols), BF16)
    zero_rows = jnp.zeros((PACK, cols), BF16)

    @pl.loop(0, bands + 1)
    def _(c):
        @pl.when(jnp.logical_not(has_low))
        def _():
            chan[c, pl.ds(0, 2 * rows)] = zero_days

        @pl.when(jnp.logical_not(has_high))
        def _():
            chan[c, pl.ds(2 * rows, 2 * rows)] = zero_days

        @pl.when(jnp.logical_not(has_up))
        def _():
            chan[c, pl.ds(strip, PACK)] = zero_rows

        @pl.when(jnp.logical_not(has_down))
        def _():
            chan[c, pl.ds(strip + PACK, PACK)] = zero_rows

    def share_rows(c):
        @pl.when(has_low)
        def _():
            later(c).wait_recv()

        @pl.when(has_high)
        def _():
            earlier(c).wait_recv()

        packed[c] = jnp.dot(
            select_m[...], chan[c, pl.ds(0, strip)], preferred_element_type=F32
        ).astype(BF16)

        far = c > 0
        by_relay = jnp.logical_and(ends_low, far), jnp.logical_and(ends_high, far)
        pl.when(jnp.logical_and(has_down, jnp.logical_not(ends_low)))(lambda: downward(c).start())
        pl.when(jnp.logical_and(has_up, jnp.logical_not(by_relay[1])))(lambda: upward(c).start())
        pl.when(by_relay[0])(lambda: depart(c, 0).start())
        pl.when(by_relay[1])(lambda: depart(c, 1).start())

    def smoothed(c):
        @pl.when(has_up)
        def _():
            downward(c).wait_recv()

        @pl.when(has_down)
        def _():
            upward(c).wait_recv()

        both = jnp.dot(smooth_m[...], chan[c], preferred_element_type=F32)
        rowed = both[:own] + both[own:]
        rowed = jnp.concatenate([rowed, jnp.zeros((own, 128), F32)], axis=1)
        across = cols + 128
        field = space_k[2] * rowed
        for k in (0, 1, 3, 4):
            field = field + space_k[k] * pltpu.roll(rowed, (2 - k) % across, 1)
        return field[:, :cols]

    def own_part(c):
        return chan[c, pl.ds(4 * rows, own + rows)].astype(F32)[:own]

    def send_to(b, k):
        peer = lax.rem(day + k, nd)
        return pltpu.make_async_remote_copy(
            src_ref=out.at[b, peer],
            dst_ref=got.at[b, day],
            send_sem=all_send.at[b],
            recv_sem=all_recv.at[b],
            device_id={"date": peer},
            device_id_type=MESH,
        )

    def fill_band(b):
        whole = own_part(b + 1) + gain[...] * smoothed(b + 1)
        for q, t in enumerate(own_order(dates)):
            strip_t = whole[q * rows : (q + 1) * rows].astype(BF16)
            filled[t, b] = strip_t
            for j in range(nd):
                out[b, j, t] = strip_t[:, j * width : (j + 1) * width]
        for k in (4, 3, 5):
            send_to(b, k).start()
        pltpu.make_async_copy(out.at[b, day], got.at[b, day], all_recv.at[b]).start()

    for c in range(AHEAD):
        share_rows(c)
        if c >= 2:
            pass_on(c - 1, 1)

    pass_on(AHEAD - 1, 1)
    pass_on(AHEAD, 1)

    at_gap = jnp.logical_or(ends_low, ends_high)

    @pl.when(ends_low)
    def _():
        pl.semaphore_wait(ready, 1)
        downward(0).start()

    @pl.when(at_gap)
    def _():
        @pl.loop(AHEAD, channels)
        def _(c):
            share_rows(c)


    gain[...] = (1.0 - own_part(0)) / (smoothed(0) + 1.0)

    @pl.loop(0, bands)
    def _(b):
        @pl.when(jnp.logical_and(b + AHEAD <= bands, jnp.logical_not(at_gap)))
        def _():
            share_rows(b + AHEAD)


        @pl.when(2 * b + AHEAD + 2 <= bands)
        def _():
            pass_on(2 * b + AHEAD + 1, 1)
            pass_on(2 * b + AHEAD + 2, 1)

        fill_band(b)

        @pl.when(b < 3)
        def _():
            pass_on(2 * b + 1, 0)
            pass_on(2 * b + 2, 0)

        pl.when(jnp.logical_and(b >= 3, b + 4 <= bands))(lambda: pass_on(b + 4, 0))

    for k in (2, 1, 6, 7):
        @pl.loop(0, bands)
        def _(b):
            send_to(b, k).start()

    fit_copy.wait()

    def project(places, pair):
        flat = [x.reshape(nd * dates * rows, width).astype(BF16) for x in pair]
        both = jnp.dot(fit[...], jnp.concatenate(flat, axis=1), preferred_element_type=F32)
        middle = TERMS * rows
        terms = both[:middle] + both[middle:]
        for i, c in enumerate(places):
            coef[c] = terms[:, i * width : (i + 1) * width].reshape(TERMS, rows, width)

    def arrived(b):
        pltpu.make_async_copy(got.at[b], got.at[b], all_recv.at[b]).wait()

    def series(b):
        return got[b].astype(F32)

    @pl.loop(0, bands // 2 - 1)
    def _(i):
        arrived(2 * i)
        arrived(2 * i + 1)
        project((2 * i, 2 * i + 1), (series(2 * i), series(2 * i + 1)))

    arrived(bands - 2)
    red, near, swir = series(2), series(6), series(8)
    savi = 1.5 * (near - red) / (near + red + 0.5)
    project((bands, bands + 1), (savi, (near - swir) / (near + swir + 0.5)))
    arrived(bands - 1)
    project((bands - 2, bands - 1), (series(bands - 2), series(bands - 1)))

    @pl.loop(0, bands + 1)
    def _(c):
        @pl.when(has_high)
        def _():
            later(c).wait_send()

        @pl.when(has_low)
        def _():
            earlier(c).wait_send()

        pl.when(has_down)(lambda: downward(c).wait_send())
        pl.when(has_up)(lambda: upward(c).wait_send())

    @pl.loop(1, channels)
    def _(c):
        for way in (0, 1):
            pl.when(passes(c, way))(lambda: arrive(c, way).wait_send())

    @pl.loop(0, bands)
    def _(b):
        sent = out.at[b, pl.ds(0, nd - 1)]
        pltpu.make_async_copy(sent, sent, all_send.at[b]).wait()


def solution(mesh):
    nd, nt = mesh.shape["date"], mesh.shape["tile"]

    def per_device(reflectance, clear_mask, time_kernel, space_kernel):
        dates, bands, rows, cols = reflectance.shape
        width = cols // nd
        own = dates * rows
        strip = 4 * rows + own + rows
        total = strip + 2 * PACK
        whole = nd * own
        anywhere = pl.BlockSpec(memory_space=pl.ANY)
        inside = pl.BlockSpec(memory_space=pltpu.VMEM)
        scalars = pl.BlockSpec(memory_space=pltpu.SMEM)
        dma = pltpu.SemaphoreType.DMA
        shapes = (
            jax.ShapeDtypeStruct((dates, bands, rows, cols), BF16),
            jax.ShapeDtypeStruct((bands + 2, TERMS, rows, width), F32),
        )
        return pl.pallas_call(
            functools.partial(kernel, (nd, nt, dates, bands, rows, cols)),
            out_shape=tuple(pltpu.VMEM(s.shape, s.dtype) for s in shapes),
            in_specs=[anywhere, anywhere, scalars, scalars, anywhere],
            out_specs=(inside, inside),
            scratch_shapes=[
                pltpu.VMEM((bands, dates, rows, cols), BF16),
                pltpu.VMEM((dates, rows, cols), jnp.int32),
                pltpu.VMEM((2 * TERMS * rows, whole), BF16),
                pltpu.VMEM((bands + 1, total, cols), BF16),
                pltpu.VMEM((bands + 1, 2 * PACK, cols), BF16),
                pltpu.VMEM((2, bands + 1, PACK, cols), BF16),
                pltpu.VMEM((own, cols), F32),
                pltpu.VMEM((bands, nd, dates, rows, width), BF16),
                pltpu.VMEM((bands, nd, dates, rows, width), BF16),
                pltpu.VMEM((2 * own, total), BF16),
                pltpu.VMEM((2 * PACK, strip), BF16),
                dma((bands + 2,)),
                dma((bands + 1, 2)),
                dma((bands + 1, 2)),
                dma((bands + 1, 2)),
                dma((bands + 1, 2)),
                dma((2, bands + 1)),
                dma((2, bands + 1)),
                dma((bands,)),
                dma((bands,)),
                pltpu.SemaphoreType.REGULAR,
            ],
            compiler_params=pltpu.CompilerParams(
                collective_id=0, has_side_effects=True, vmem_limit_bytes=56 * 2**20
            ),
            name="fill_and_fit",
        )(
            reflectance,
            clear_mask,
            time_kernel,
            space_kernel,
            jnp.asarray(fit_operand(nd * dates, rows)),
        )

    placed = (P("date", None, "tile", None), P("date", "tile", None), P(), P())
    return jax.shard_map(
        per_device,
        mesh=mesh,
        in_specs=placed,
        out_specs=(P("date", None, "tile", None), P(None, None, "tile", "date")),
        check_vma=False,
    )
```

```python
import functools
import math

import jax
import jax.numpy as jnp
import numpy as np
from jax import lax
from jax.experimental import pallas as pl
from jax.experimental.pallas import tpu as pltpu
from jax.sharding import PartitionSpec as P

TERMS = 24
PACK = 32
AHEAD = 4
MESH = pl.DeviceIdType.MESH
F32 = jnp.float32
BF16 = jnp.bfloat16


def fit_matrix(dates, terms):
    steps = np.arange(dates, dtype=np.float64)
    columns = [np.ones((dates,)), steps / dates - 0.5]
    for order in range(1, (terms - 2) // 2 + 1):
        angle = 2.0 * math.pi * order * steps / dates
        columns.append(np.cos(angle))
        columns.append(np.sin(angle))
    basis = np.stack(columns, axis=1)
    factor = np.linalg.cholesky(basis.T @ basis)
    return np.linalg.solve(factor.T, np.linalg.solve(factor, basis.T))


def fit_operand(dates, rows):
    wide = np.kron(fit_matrix(dates, TERMS), np.eye(rows)).astype(np.float32)
    high = wide.astype(BF16)
    rest = (wide - high.astype(np.float32)).astype(BF16)
    return np.concatenate([high, rest], axis=0)


def own_order(dates):
    return [0, 1, dates - 2, dates - 1] + list(range(2, dates - 2))


def strip_rows(n, dates):
    q = n >> 3
    date = jnp.where(q < 4 + dates, q - 6, -100)
    date = jnp.where(q < 8, q - 8 + dates, date)
    date = jnp.where(q < 6, q - 4, date)
    date = jnp.where(q < 4, q - 2 + dates, date)
    date = jnp.where(q < 2, q - 2, date)
    return date, n & 7


def halo_rows(m, dates, low, high):
    at = m & (PACK - 1)
    date = jnp.where(at < 2 * (dates + 4), (at >> 1) - 2, -200)
    return date, (at & 1) + jnp.where(m < PACK, low, high)


def relay(c, way, half, channels):
    return 2 * (c + 1) + way if half >= 2 * (channels + 2) else 1


def kernel(
    sizes,
    refl, mask, time_k, space_k, fit_in,
    filled, coef,
    raw, cloud, fit, chan, packed, hold, gain, out, got, smooth_m, select_m,
    in_sem, date_send, date_recv, row_send, row_recv, hop_send, hop_recv,
    all_send, all_recv, ready,
):
    nd, nt, dates, bands, rows, cols = sizes
    width = cols // nd
    own = dates * rows
    strip = 4 * rows + own + rows
    total = strip + 2 * PACK
    day = lax.axis_index("date")
    tile = lax.axis_index("tile")
    has_low, has_high = day > 0, day < nd - 1
    has_up, has_down = tile > 0, tile < nt - 1
    half = nt // 2
    ends_low, ends_high = tile == half - 1, tile == half
    channels = bands + 1

    def passes(c, way):
        return tile == (half if way else 0) + relay(c, way, half, channels)

    def band_in(b):
        return pltpu.make_async_copy(refl.at[:, b], raw.at[b], in_sem.at[b])

    mask_in = pltpu.make_async_copy(mask, cloud, in_sem.at[bands])
    fit_copy = pltpu.make_async_copy(fit_in, fit, in_sem.at[bands + 1])
    barrier = pltpu.get_barrier_semaphore()
    for k in range(1, nd):
        pl.semaphore_signal(
            barrier, inc=1, device_id={"date": lax.rem(day + k, nd)}, device_id_type=MESH
        )

    def greet(strip):
        pl.semaphore_signal(barrier, inc=1, device_id={"tile": strip}, device_id_type=MESH)

    mask_in.start()

    @pl.loop(0, bands)
    def _(b):
        band_in(b).start()

    fit_copy.start()

    pl.when(jnp.logical_and(has_up, tile != half))(lambda: greet(tile - 1))
    pl.when(has_down)(lambda: greet(tile + 1))
    greeted = jnp.where(has_up, 1, 0)
    greeted = greeted + jnp.where(jnp.logical_and(has_down, tile != half - 1), 1, 0)
    greeted = greeted + jnp.where(ends_low, bands, 0) + jnp.where(ends_high, 2 * bands, 0)

    @pl.loop(1, channels)
    def _(c):
        @pl.when(passes(c, 0))
        def _():
            greet(half - 1)
            greet(half)

        pl.when(passes(c, 1))(lambda: greet(half))
        pl.when(ends_low)(lambda: greet(half + relay(c, 1, half, channels)))

    def count(c, total):
        return total + jnp.where(passes(c, 1), 1, 0)

    greeted = lax.fori_loop(1, channels, count, greeted)

    def tell_ready(strip):
        pl.semaphore_signal(ready, inc=1, device_id={"tile": strip}, device_id_type=MESH)

    def later(c):
        return pltpu.make_async_remote_copy(
            src_ref=chan.at[c, pl.ds(6 * rows, 2 * rows)],
            dst_ref=chan.at[c, pl.ds(0, 2 * rows)],
            send_sem=date_send.at[c, 0],
            recv_sem=date_recv.at[c, 0],
            device_id={"date": jnp.minimum(day + 1, nd - 1)},
            device_id_type=MESH,
        )

    def earlier(c):
        return pltpu.make_async_remote_copy(
            src_ref=chan.at[c, pl.ds(4 * rows, 2 * rows)],
            dst_ref=chan.at[c, pl.ds(2 * rows, 2 * rows)],
            send_sem=date_send.at[c, 1],
            recv_sem=date_recv.at[c, 1],
            device_id={"date": jnp.maximum(day - 1, 0)},
            device_id_type=MESH,
        )

    def downward(c):
        return pltpu.make_async_remote_copy(
            src_ref=packed.at[c, pl.ds(0, PACK)],
            dst_ref=chan.at[c, pl.ds(strip, PACK)],
            send_sem=row_send.at[c, 0],
            recv_sem=row_recv.at[c, 0],
            device_id={"tile": jnp.minimum(tile + 1, nt - 1)},
            device_id_type=MESH,
        )

    def upward(c):
        return pltpu.make_async_remote_copy(
            src_ref=packed.at[c, pl.ds(PACK, PACK)],
            dst_ref=chan.at[c, pl.ds(strip + PACK, PACK)],
            send_sem=row_send.at[c, 1],
            recv_sem=row_recv.at[c, 1],
            device_id={"tile": jnp.maximum(tile - 1, 0)},
            device_id_type=MESH,
        )

    def depart(c, way):
        return pltpu.make_async_remote_copy(
            src_ref=packed.at[c, pl.ds(way * PACK, PACK)],
            dst_ref=hold.at[way, c],
            send_sem=row_send.at[c, way],
            recv_sem=hop_recv.at[way, c],
            device_id={"tile": (half if way else 0) + relay(c, way, half, channels)},
            device_id_type=MESH,
        )

    def arrive(c, way):
        return pltpu.make_async_remote_copy(
            src_ref=hold.at[way, c],
            dst_ref=chan.at[c, pl.ds(strip + way * PACK, PACK)],
            send_sem=hop_send.at[way, c],
            recv_sem=row_recv.at[c, way],
            device_id={"tile": half - 1 if way else half},
            device_id_type=MESH,
        )

    def pass_on(c, way):
        @pl.when(passes(c, way))
        def _():
            depart(c, way).wait_recv()
            if way == 0:
                pl.semaphore_wait(ready, 1)
            arrive(c, way).start()

    def send_dates(c):
        @pl.when(has_high)
        def _():
            later(c).start()

        @pl.when(has_low)
        def _():
            earlier(c).start()

    blank = jnp.zeros((rows, cols), F32)

    def store_own(c, values):
        parts = [values(t) for t in own_order(dates)] + [blank]
        chan[c, pl.ds(4 * rows, own + rows)] = jnp.concatenate(parts, axis=0).astype(BF16)

    mask_in.wait()
    store_own(0, lambda t: cloud[t].astype(F32))
    pl.semaphore_wait(barrier, nd - 1 + greeted)

    @pl.when(ends_high)
    def _():
        tell_ready(half - 1)

        @pl.loop(1, channels)
        def _(c):
            tell_ready(relay(c, 0, half, channels))

    send_dates(0)

    @pl.loop(0, bands)
    def _(b):
        band_in(b).wait()
        store_own(b + 1, lambda t: raw[b, t].astype(F32) * cloud[t].astype(F32))
        send_dates(b + 1)

    at_out = lax.broadcasted_iota(jnp.int32, (own, total), 0)
    at_in = lax.broadcasted_iota(jnp.int32, (own, total), 1)
    q = at_out >> 3
    date_out = jnp.where(q < 2, q, jnp.where(q < 4, q - 4 + dates, q - 2))
    row_out = at_out & 7
    date_a, row_a = strip_rows(at_in, dates)
    date_b, row_b = halo_rows(at_in - strip, dates, -2, rows)
    inside = at_in < strip
    apart = jnp.where(inside, date_a, date_b) - date_out
    below = jnp.where(inside, row_a, row_b) - row_out
    weight_t = jnp.zeros((own, total), F32)
    weight_r = jnp.zeros((own, total), F32)
    for k in range(5):
        weight_t = weight_t + jnp.where(apart == k - 2, time_k[k], 0.0)
        weight_r = weight_r + jnp.where(below == k - 2, space_k[k], 0.0)
    weight = weight_t * weight_r
    weight_hi = weight.astype(BF16).astype(F32)
    smooth_m[...] = jnp.concatenate([weight_hi, weight - weight_hi], axis=0).astype(BF16)

    pick = lax.broadcasted_iota(jnp.int32, (2 * PACK, strip), 0)
    date_p, row_p = halo_rows(pick, dates, rows - 2, 0)
    date_s, row_s = strip_rows(lax.broadcasted_iota(jnp.int32, (2 * PACK, strip), 1), dates)
    hit = jnp.logical_and(date_p == date_s, row_p == row_s)
    select_m[...] = jnp.where(hit, 1.0, 0.0).astype(BF16)

    zero_days = jnp.zeros((2 * rows, cols), BF16)
    zero_rows = jnp.zeros((PACK, cols), BF16)

    @pl.loop(0, bands + 1)
    def _(c):
        @pl.when(jnp.logical_not(has_low))
        def _():
            chan[c, pl.ds(0, 2 * rows)] = zero_days

        @pl.when(jnp.logical_not(has_high))
        def _():
            chan[c, pl.ds(2 * rows, 2 * rows)] = zero_days

        @pl.when(jnp.logical_not(has_up))
        def _():
            chan[c, pl.ds(strip, PACK)] = zero_rows

        @pl.when(jnp.logical_not(has_down))
        def _():
            chan[c, pl.ds(strip + PACK, PACK)] = zero_rows

    def share_rows(c):
        @pl.when(has_low)
        def _():
            later(c).wait_recv()

        @pl.when(has_high)
        def _():
            earlier(c).wait_recv()

        packed[c] = jnp.dot(
            select_m[...], chan[c, pl.ds(0, strip)], preferred_element_type=F32
        ).astype(BF16)

        far = c > 0
        by_relay = jnp.logical_and(ends_low, far), jnp.logical_and(ends_high, far)
        pl.when(jnp.logical_and(has_down, jnp.logical_not(ends_low)))(lambda: downward(c).start())
        pl.when(jnp.logical_and(has_up, jnp.logical_not(by_relay[1])))(lambda: upward(c).start())
        pl.when(by_relay[0])(lambda: depart(c, 0).start())
        pl.when(by_relay[1])(lambda: depart(c, 1).start())

    def smoothed(c):
        @pl.when(has_up)
        def _():
            downward(c).wait_recv()

        @pl.when(has_down)
        def _():
            upward(c).wait_recv()

        both = jnp.dot(smooth_m[...], chan[c], preferred_element_type=F32)
        rowed = both[:own] + both[own:]
        rowed = jnp.concatenate([rowed, jnp.zeros((own, 128), F32)], axis=1)
        across = cols + 128
        field = space_k[2] * rowed
        for k in (0, 1, 3, 4):
            field = field + space_k[k] * pltpu.roll(rowed, (2 - k) % across, 1)
        return field[:, :cols]

    def own_part(c):
        return chan[c, pl.ds(4 * rows, own + rows)].astype(F32)[:own]

    def send_to(b, k):
        peer = lax.rem(day + k, nd)
        return pltpu.make_async_remote_copy(
            src_ref=out.at[b, peer],
            dst_ref=got.at[b, day],
            send_sem=all_send.at[b],
            recv_sem=all_recv.at[b],
            device_id={"date": peer},
            device_id_type=MESH,
        )

    def fill_band(b):
        whole = own_part(b + 1) + gain[...] * smoothed(b + 1)
        for q, t in enumerate(own_order(dates)):
            strip_t = whole[q * rows : (q + 1) * rows].astype(BF16)
            filled[t, b] = strip_t
            for j in range(nd):
                out[b, j, t] = strip_t[:, j * width : (j + 1) * width]
        for k in (4, 3, 5):
            send_to(b, k).start()
        pltpu.make_async_copy(out.at[b, day], got.at[b, day], all_recv.at[b]).start()

    for c in range(AHEAD):
        share_rows(c)
        if c >= 2:
            pass_on(c - 1, 1)

    pass_on(AHEAD - 1, 1)
    pass_on(AHEAD, 1)

    at_gap = jnp.logical_or(ends_low, ends_high)

    @pl.when(ends_low)
    def _():
        pl.semaphore_wait(ready, 1)
        downward(0).start()

    @pl.when(at_gap)
    def _():
        @pl.loop(AHEAD, channels)
        def _(c):
            share_rows(c)


    gain[...] = (1.0 - own_part(0)) / (smoothed(0) + 1.0)

    @pl.loop(0, bands)
    def _(b):
        @pl.when(jnp.logical_and(b + AHEAD <= bands, jnp.logical_not(at_gap)))
        def _():
            share_rows(b + AHEAD)


        @pl.when(2 * b + AHEAD + 2 <= bands)
        def _():
            pass_on(2 * b + AHEAD + 1, 1)
            pass_on(2 * b + AHEAD + 2, 1)

        fill_band(b)

        @pl.when(b < 3)
        def _():
            pass_on(2 * b + 1, 0)
            pass_on(2 * b + 2, 0)

        pl.when(jnp.logical_and(b >= 3, b + 4 <= bands))(lambda: pass_on(b + 4, 0))

    for k in (2, 1, 6, 7):
        @pl.loop(0, bands)
        def _(b):
            send_to(b, k).start()

    fit_copy.wait()

    def project(places, pair):
        flat = [x.reshape(nd * dates * rows, width).astype(BF16) for x in pair]
        both = jnp.dot(fit[...], jnp.concatenate(flat, axis=1), preferred_element_type=F32)
        middle = TERMS * rows
        terms = both[:middle] + both[middle:]
        for i, c in enumerate(places):
            coef[c] = terms[:, i * width : (i + 1) * width].reshape(TERMS, rows, width)

    def arrived(b):
        pltpu.make_async_copy(got.at[b], got.at[b], all_recv.at[b]).wait()

    def series(b):
        return got[b].astype(F32)

    @pl.loop(0, bands // 2 - 1)
    def _(i):
        arrived(2 * i)
        arrived(2 * i + 1)
        project((2 * i, 2 * i + 1), (series(2 * i), series(2 * i + 1)))

    arrived(bands - 2)
    red, near, swir = series(2), series(6), series(8)
    savi = 1.5 * (near - red) / (near + red + 0.5)
    project((bands, bands + 1), (savi, (near - swir) / (near + swir + 0.5)))
    arrived(bands - 1)
    project((bands - 2, bands - 1), (series(bands - 2), series(bands - 1)))

    @pl.loop(0, bands + 1)
    def _(c):
        @pl.when(has_high)
        def _():
            later(c).wait_send()

        @pl.when(has_low)
        def _():
            earlier(c).wait_send()

        pl.when(has_down)(lambda: downward(c).wait_send())
        pl.when(has_up)(lambda: upward(c).wait_send())

    @pl.loop(1, channels)
    def _(c):
        for way in (0, 1):
            pl.when(passes(c, way))(lambda: arrive(c, way).wait_send())

    @pl.loop(0, bands)
    def _(b):
        sent = out.at[b, pl.ds(0, nd - 1)]
        pltpu.make_async_copy(sent, sent, all_send.at[b]).wait()


def hand_over(filled_in, coef_in, filled, coef, sem):
    copies = [
        pltpu.make_async_copy(filled_in, filled, sem.at[0]),
        pltpu.make_async_copy(coef_in, coef, sem.at[1]),
    ]
    for copy in copies:
        copy.start()
    for copy in copies:
        copy.wait()


def solution(mesh):
    nd, nt = mesh.shape["date"], mesh.shape["tile"]

    def per_device(reflectance, clear_mask, time_kernel, space_kernel):
        dates, bands, rows, cols = reflectance.shape
        width = cols // nd
        own = dates * rows
        strip = 4 * rows + own + rows
        total = strip + 2 * PACK
        whole = nd * own
        anywhere = pl.BlockSpec(memory_space=pl.ANY)
        inside = pl.BlockSpec(memory_space=pltpu.VMEM)
        scalars = pl.BlockSpec(memory_space=pltpu.SMEM)
        dma = pltpu.SemaphoreType.DMA
        shapes = (
            jax.ShapeDtypeStruct((dates, bands, rows, cols), BF16),
            jax.ShapeDtypeStruct((bands + 2, TERMS, rows, width), F32),
        )
        results = pl.pallas_call(
            functools.partial(kernel, (nd, nt, dates, bands, rows, cols)),
            out_shape=tuple(pltpu.VMEM(s.shape, s.dtype) for s in shapes),
            in_specs=[anywhere, anywhere, scalars, scalars, anywhere],
            out_specs=(inside, inside),
            scratch_shapes=[
                pltpu.VMEM((bands, dates, rows, cols), BF16),
                pltpu.VMEM((dates, rows, cols), jnp.int32),
                pltpu.VMEM((2 * TERMS * rows, whole), BF16),
                pltpu.VMEM((bands + 1, total, cols), BF16),
                pltpu.VMEM((bands + 1, 2 * PACK, cols), BF16),
                pltpu.VMEM((2, bands + 1, PACK, cols), BF16),
                pltpu.VMEM((own, cols), F32),
                pltpu.VMEM((bands, nd, dates, rows, width), BF16),
                pltpu.VMEM((bands, nd, dates, rows, width), BF16),
                pltpu.VMEM((2 * own, total), BF16),
                pltpu.VMEM((2 * PACK, strip), BF16),
                dma((bands + 2,)),
                dma((bands + 1, 2)),
                dma((bands + 1, 2)),
                dma((bands + 1, 2)),
                dma((bands + 1, 2)),
                dma((2, bands + 1)),
                dma((2, bands + 1)),
                dma((bands,)),
                dma((bands,)),
                pltpu.SemaphoreType.REGULAR,
            ],
            compiler_params=pltpu.CompilerParams(
                collective_id=0, has_side_effects=True, vmem_limit_bytes=56 * 2**20
            ),
            name="fill_and_fit",
        )(
            reflectance,
            clear_mask,
            time_kernel,
            space_kernel,
            jnp.asarray(fit_operand(nd * dates, rows)),
        )
        return pl.pallas_call(
            hand_over,
            out_shape=shapes,
            in_specs=[anywhere, anywhere],
            out_specs=(anywhere, anywhere),
            scratch_shapes=[dma((2,))],
            compiler_params=pltpu.CompilerParams(vmem_limit_bytes=2**20),
            name="hand_over",
        )(*results)

    placed = (P("date", None, "tile", None), P("date", "tile", None), P(), P())
    return jax.shard_map(
        per_device,
        mesh=mesh,
        in_specs=placed,
        out_specs=(P("date", None, "tile", None), P(None, None, "tile", "date")),
        check_vma=False,
    )
```
